512 devices in a mesh: prow: 32 (over z, x), pcol: 16 (over y, core).
Axes of the slice: x: 4, y: 8, z: 8, core: 2. Of those that a mesh axis runs over, the one named last changes fastest.
Arguments:
- trailing: float32 [16384, 16384], P('prow', 'pcol'), may hold values from -48 to 48, as said below
- panel: float32 [16384, 256], P('prow', 'pcol'), may hold values from -48 to 48, as said below
Outputs:
- updated: float32 [16384, 16384], P('prow', 'pcol')
- basis_out: float32 [16384, 256], P('prow')
The draws below stay inside these ranges and needn't reach their ends.
Inputs may be any that keep to these rules, and one draw needn't show every extreme that they name: trailing is exactly symmetric, with a positive added diagonal. panel has full column rank.
All inputs are finite; a program needn't handle non-finite values.
Results may differ from the reference program's by a relative error of at most 0.000096.
Values sent between devices are 32-bit elements; how exact they have to be, the bound alone decides.
No kernel may reach another device: no remote copies, remote signals or barrier semaphores. Data moves between devices by JAX's collectives and lax.ppermute only.
A program may use at most 64 MiB of HBM per device.

```python
import math
import jax
import jax.numpy as jnp
from jax import lax

PANEL = 256
ORDER = 16384


def draw_trailing(key, part):
    key = jax.random.fold_in(key, 11)
    noise_key = jax.random.fold_in(key, 0)
    noise = jax.random.normal(noise_key, (ORDER, ORDER), jnp.float32)
    symmetric = (noise + noise.T) * math.sqrt(0.5)
    index_rows = lax.broadcasted_iota(jnp.int32, (ORDER, ORDER), 0)
    index_cols = lax.broadcasted_iota(jnp.int32, (ORDER, ORDER), 1)
    diagonal = jnp.where(index_rows == index_cols, 4.0, 0.0).astype(jnp.float32)
    return jnp.clip(symmetric + diagonal, -48.0, 48.0)


def draw_panel(key, part):
    key = jax.random.fold_in(key, 23)
    noise_key = jax.random.fold_in(key, 0)
    values = jax.random.normal(noise_key, (ORDER, PANEL), jnp.float32)
    return jnp.clip(values, -48.0, 48.0)


def setup_inputs(seed: int = 0) -> dict:
    keys = jax.random.split(jax.random.key(seed), 3)
    return {
        "trailing": draw_trailing(jax.random.fold_in(keys[2], 71), 0),
        "panel": draw_panel(jax.random.fold_in(keys[2], 71), 0),
    }


def matmul(left, right):
    return jnp.dot(left.astype(jnp.float32), right.astype(jnp.float32), precision=lax.Precision.HIGHEST, preferred_element_type=jnp.float32)

def reference(trailing, panel):
    gram = matmul(panel.T, panel)
    factor = jnp.linalg.cholesky(gram)
    basis_out = lax.linalg.triangular_solve(factor, panel, left_side=False, lower=True, transpose_a=True)
    product = matmul(trailing, basis_out)
    projected = matmul(basis_out.T, product)
    correction = product - 0.5 * matmul(basis_out, projected)
    updated = trailing - matmul(basis_out, correction.T) - matmul(correction, basis_out.T)
    return (updated, basis_out)
```

```python
import jax
import jax.numpy as jnp
from jax import lax
from jax.sharding import Mesh, PartitionSpec as P

ROWS = ("z", "x")
COLS = ("y", "c")
ALL = ("z", "x", "y", "c")
BLOCK = 32


def matmul(left, right, contract, precision=lax.Precision.HIGHEST):
    return lax.dot_general(
        left, right, ((contract[:1], contract[1:]), ((), ())),
        precision=precision, preferred_element_type=jnp.float32,
    )


def exchange(value, axis):
    return lax.all_to_all(value, axis, 0, 0, tiled=True)


def repeat(value, count):
    return jnp.broadcast_to(value[None], (count, *value.shape))


def blocks_of_columns():
    pairs = []
    for z in range(8):
        for x in range(4):
            for col in range(16):
                part = 8 * x + z
                row = 2 * col + part // 16
                pairs.append((row * 16 + part % 16, (z * 4 + x) * 16 + col))
    return pairs


def shards(trailing, panel):
    order = panel.shape[0] // BLOCK
    width = panel.shape[1] * order
    column = lax.axis_index(COLS)
    pairs = blocks_of_columns()
    high = lax.Precision.HIGH

    panel_rows = lax.all_gather(panel, COLS, axis=1, tiled=True)
    block = lax.dynamic_slice(panel_rows, (column * BLOCK, 0), (BLOCK, width))
    panel_block = lax.ppermute(block, ALL, pairs)

    partial = matmul(trailing, panel_rows, (0, 0), high)
    partial = lax.optimization_barrier((partial, panel_block))[0]
    partial = exchange(partial.reshape(4, 256, width), "x").sum(0)
    product_block = exchange(partial.reshape(8, BLOCK, width), "z").sum(0)

    both = jnp.concatenate([product_block, panel_block], 1)
    both = exchange(repeat(both, 8), "z").reshape(256, 2 * width)
    both_cols = exchange(repeat(both, 4), "x").reshape(1024, 2 * width)

    back = lax.ppermute(product_block, ALL, [(b, a) for a, b in pairs])

    small = matmul(both_cols[:, width:], both_cols, (0, 0))
    cross, gram = small[:, :width], small[:, width:]
    row_ids = lax.broadcasted_iota(jnp.int32, (width, width), 0)
    col_ids = lax.broadcasted_iota(jnp.int32, (width, width), 1)
    packed = jnp.where(col_ids <= row_ids, gram, cross).reshape(16, 16, width)
    diagonal = jnp.sum(jnp.where(col_ids == row_ids, cross, 0.0), 1).reshape(16, 1, 16)
    diagonal = jnp.pad(diagonal, ((0, 0), (0, 0), (0, width - 16)))
    packed = jnp.concatenate([packed, diagonal], 1)
    packed, back = lax.optimization_barrier((packed, back))
    packed = exchange(packed, COLS).sum(0)

    gathered = lax.all_gather(jnp.concatenate([back, packed], 0), COLS, axis=0)
    product_rows = gathered[:, :BLOCK].reshape(512, width)
    packed = gathered[:, BLOCK : BLOCK + 16].reshape(width, width)
    diagonal = gathered[:, BLOCK + 16, :16].reshape(width, 1)
    flipped = packed.T
    gram = jnp.where(col_ids <= row_ids, packed, flipped)
    cross = jnp.where(col_ids > row_ids, packed, jnp.where(col_ids == row_ids, diagonal, flipped))

    factor = jnp.linalg.cholesky(gram)
    inverse = lax.linalg.triangular_solve(
        factor, jnp.eye(width, dtype=jnp.float32), left_side=True, lower=True
    )
    basis_rows = matmul(panel_rows, inverse, (1, 1))
    left = matmul(basis_rows, inverse, (1, 0))
    right = product_rows - matmul(left, cross, (1, 0))
    right = matmul(matmul(right, inverse, (1, 1)), inverse, (1, 0))
    updated = trailing - matmul(jnp.concatenate([left, right], 1), both_cols, (1, 1), high)
    return (updated, basis_rows)


def solution(mesh):
    fine = Mesh(mesh.devices.reshape(8, 4, 8, 2), ALL)
    return jax.shard_map(
        shards, mesh=fine, in_specs=(P(ROWS, COLS), P(ROWS, COLS)),
        out_specs=(P(ROWS, COLS), P(ROWS, None)), check_vma=False,
    )
```

```python
import jax
import jax.numpy as jnp
from jax import lax
from jax.experimental import pallas as pl
from jax.experimental.pallas import tpu as pltpu
from jax.sharding import Mesh, PartitionSpec as P

ROWS = ("z", "x")
COLS = ("y", "c")
ALL = ("z", "x", "y", "c")
BLOCK = 32


def matmul(left, right, contract, precision=lax.Precision.HIGHEST):
    return lax.dot_general(
        left, right, ((contract[:1], contract[1:]), ((), ())),
        precision=precision, preferred_element_type=jnp.float32,
    )


def iota(shape, dimension):
    return lax.broadcasted_iota(jnp.int32, shape, dimension)


def whole(value):
    return jnp.broadcast_to(value, (8, 128))


def inverse_of_block(tile, offset, size):
    start = 0 if offset else size
    lane, row = iota((size, 128), 1), iota((size, 128), 0)
    inside = (lane >= offset) & (lane < offset + size)
    work = jnp.where(inside, tile, jnp.where(lane == row + start, 1.0, 0.0))
    count = size // 8
    parts = [work[8 * i : 8 * i + 8] for i in range(count)]
    sub = iota((8, 128), 0)
    done = []
    for q in range(count):
        first = offset + 8 * q
        cols = [
            [whole(part[:, first + j : first + j + 1]) for j in range(8)]
            for part in parts[q:]
        ]
        pivots = {(i, j): whole(cols[0][j][i : i + 1]) for j in range(8) for i in range(j, 8)}
        rows = [whole(parts[q][i : i + 1]) for i in range(8)]
        inverses = []
        for j in range(8):
            inverses.append(1.0 / pivots[j, j])
            factors = {i: pivots[i, j] * inverses[j] for i in range(j + 1, 8)}
            for m in range(j + 1, 8):
                for i in range(m, 8):
                    pivots[i, m] = pivots[i, m] - factors[i] * pivots[m, j]
            for i in range(j + 1, 8):
                rows[i] = rows[i] - factors[i] * rows[j]
                for part in cols[1:]:
                    part[i] = part[i] - factors[i] * part[j]
        scaled = [row_j * inverse for row_j, inverse in zip(rows, inverses)]
        for i in range(q + 1, count):
            total = cols[i - q][0] * scaled[0]
            for j in range(1, 8):
                total = total + cols[i - q][j] * scaled[j]
            parts[i] = parts[i] - total
        final = rows[0] / jnp.sqrt(pivots[0, 0])
        for j in range(1, 8):
            final = jnp.where(sub == j, rows[j] / jnp.sqrt(pivots[j, j]), final)
        done.append(final)
    return jnp.concatenate(done, 0)[:, start : start + size]


def finish_kernel(gathered_ref, panel_ref, basis_ref, left_ref, work_ref, inverse_ref):
    width = panel_ref.shape[0]
    panel = panel_ref[...]
    packed = jnp.concatenate([gathered_ref[j, BLOCK : BLOCK + 16] for j in range(16)], 0)
    diagonal = gathered_ref[0, BLOCK + 16 : BLOCK + 17]
    for j in range(1, 16):
        diagonal = diagonal + gathered_ref[j, BLOCK + 16 : BLOCK + 17]
    row, col = iota((width, width), 0), iota((width, width), 1)
    flipped = packed.T
    work_ref[:, :width] = jnp.where(col <= row, packed, flipped)
    work_ref[:, width:] = jnp.where(col == row, 1.0, 0.0)
    size = 64
    for k in range(0, width, size):
        tile = k // 128 * 128
        block = inverse_of_block(work_ref[k : k + size, tile : tile + 128], k - tile, size)
        rows = matmul(block, work_ref[k : k + size, :], (1, 0))
        inverse_ref[k : k + size, :] = rows[:, width:]
        if k + size < width:
            below = matmul(rows[:, k + size : width], rows, (0, 0))
            work_ref[k + size :, :] = work_ref[k + size :, :] - below
    cross = jnp.where(col > row, packed, jnp.where(col == row, diagonal, flipped))
    inverse = inverse_ref[...]
    whole_inverse = matmul(inverse, inverse, (0, 0))
    product = jnp.concatenate([gathered_ref[j, :BLOCK] for j in range(16)], 0)
    basis_ref[...] = matmul(panel, inverse, (0, 1))
    left = matmul(panel, whole_inverse, (0, 0))
    left_ref[:, :width] = left
    left_ref[:, width:] = matmul(product - matmul(left, cross, (1, 0)), whole_inverse, (1, 0))


def finish(gathered, panel):
    width, rows = panel.shape
    return pl.pallas_call(
        finish_kernel,
        out_shape=(
            jax.ShapeDtypeStruct((rows, width), jnp.float32),
            jax.ShapeDtypeStruct((rows, 2 * width), jnp.float32),
        ),
        scratch_shapes=[
            pltpu.VMEM((width, 2 * width), jnp.float32),
            pltpu.VMEM((width, width), jnp.float32),
        ],
        compiler_params=pltpu.CompilerParams(vmem_limit_bytes=32 * 2**20),
        cost_estimate=pl.CostEstimate(flops=2 * 10**9, bytes_accessed=4 * 10**6, transcendentals=0),
        name="finish",
    )(gathered, panel)


def exchange(value, axis):
    return lax.all_to_all(value, axis, 0, 0, tiled=True)


def repeat(value, count):
    return jnp.broadcast_to(value[None], (count, *value.shape))


def blocks_of_columns():
    pairs = []
    for z in range(8):
        for x in range(4):
            for col in range(16):
                part = 8 * x + z
                row = 2 * col + part // 16
                pairs.append((row * 16 + part % 16, (z * 4 + x) * 16 + col))
    return pairs


def shards(trailing, panel):
    width = panel.shape[1] * lax.axis_size(COLS)
    column = lax.axis_index(COLS)
    pairs = blocks_of_columns()
    high = lax.Precision.HIGH

    panel_rows = lax.all_gather(panel, COLS, axis=1, tiled=True)
    block = lax.dynamic_slice(panel_rows, (column * BLOCK, 0), (BLOCK, width))
    panel_block = lax.ppermute(block, ALL, pairs)

    partial = matmul(trailing, panel_rows, (0, 0), high)
    partial = lax.optimization_barrier((partial, panel_block))[0]
    partial = exchange(partial.reshape(4, 256, width), "x").sum(0)
    product_block = exchange(partial.reshape(8, BLOCK, width), "z").sum(0)

    both = jnp.concatenate([product_block, panel_block], 1)
    both = exchange(repeat(both, 8), "z").reshape(256, 2 * width)
    both_cols = exchange(repeat(both, 4), "x").reshape(1024, 2 * width)

    back = lax.ppermute(product_block, ALL, [(b, a) for a, b in pairs])

    small = matmul(both_cols[:, width:], both_cols, (0, 0))
    cross, gram = small[:, :width], small[:, width:]
    row, col = iota((width, width), 0), iota((width, width), 1)
    packed = jnp.where(col <= row, gram, cross).reshape(16, 16, width)
    diagonal = jnp.sum(jnp.where(col == row, cross, 0.0), 0)
    own = iota((16, 1, width), 0) == iota((16, 1, width), 2) // 16
    packed = jnp.concatenate([packed, jnp.where(own, diagonal, 0.0)], 1)
    packed, back = lax.optimization_barrier((packed, back))
    packed = exchange(packed, COLS).sum(0)

    gathered = lax.all_gather(jnp.concatenate([back, packed], 0), COLS, axis=0)
    basis_rows, left = finish(gathered, panel_rows.T)
    updated = trailing - matmul(left, both_cols, (1, 1), high)
    return (updated, basis_rows)


def solution(mesh):
    fine = Mesh(mesh.devices.reshape(8, 4, 8, 2), ALL)
    return jax.shard_map(
        shards, mesh=fine, in_specs=(P(ROWS, COLS), P(ROWS, COLS)),
        out_specs=(P(ROWS, COLS), P(ROWS, None)), check_vma=False,
    )
```

```python
import jax
import jax.numpy as jnp
from jax import lax
from jax.experimental import pallas as pl
from jax.experimental.pallas import tpu as pltpu
from jax.sharding import Mesh, PartitionSpec as P

ROWS = ("z", "x")
COLS = ("y", "c")
ALL = ("z", "x", "y", "c")
BLOCK = 32


def matmul(left, right, contract, precision=lax.Precision.HIGHEST):
    return lax.dot_general(
        left, right, ((contract[:1], contract[1:]), ((), ())),
        precision=precision, preferred_element_type=jnp.float32,
    )


def iota(shape, dimension):
    return lax.broadcasted_iota(jnp.int32, shape, dimension)


def whole(value):
    return jnp.broadcast_to(value, (8, 128))


def inverse_of_block(tile, offset, size):
    start = 0 if offset else size
    lane, row = iota((size, 128), 1), iota((size, 128), 0)
    inside = (lane >= offset) & (lane < offset + size)
    work = jnp.where(inside, tile, jnp.where(lane == row + start, 1.0, 0.0))
    count = size // 8
    parts = [work[8 * i : 8 * i + 8] for i in range(count)]
    sub = iota((8, 128), 0)
    done = []
    for q in range(count):
        first = offset + 8 * q
        cols = [
            [whole(part[:, first + j : first + j + 1]) for j in range(8)]
            for part in parts[q:]
        ]
        pivots = {(i, j): whole(cols[0][j][i : i + 1]) for j in range(8) for i in range(j, 8)}
        rows = [whole(parts[q][i : i + 1]) for i in range(8)]
        inverses = []
        for j in range(8):
            inverses.append(1.0 / pivots[j, j])
            factors = {i: pivots[i, j] * inverses[j] for i in range(j + 1, 8)}
            for m in range(j + 1, 8):
                for i in range(m, 8):
                    pivots[i, m] = pivots[i, m] - pivots[i, j] * pivots[m, j] * inverses[j]
            for i in range(j + 1, 8):
                rows[i] = rows[i] - factors[i] * rows[j]
                for part in cols[1:]:
                    part[i] = part[i] - factors[i] * part[j]
        scaled = [row_j * inverse for row_j, inverse in zip(rows, inverses)]
        for i in range(q + 1, count):
            total = cols[i - q][0] * scaled[0]
            for j in range(1, 8):
                total = total + cols[i - q][j] * scaled[j]
            parts[i] = parts[i] - total
        final = rows[0] / jnp.sqrt(pivots[0, 0])
        for j in range(1, 8):
            final = jnp.where(sub == j, rows[j] / jnp.sqrt(pivots[j, j]), final)
        done.append(final)
    return jnp.concatenate(done, 0)[:, start : start + size]


def finish_kernel(gathered_ref, panel_ref, basis_ref, left_ref, work_ref, inverse_ref):
    width = panel_ref.shape[0]
    panel = panel_ref[...]
    packed = jnp.concatenate([gathered_ref[j, BLOCK : BLOCK + 16] for j in range(16)], 0)
    diagonal = gathered_ref[0, BLOCK + 16 : BLOCK + 17]
    for j in range(1, 16):
        diagonal = diagonal + gathered_ref[j, BLOCK + 16 : BLOCK + 17]
    row, col = iota((width, width), 0), iota((width, width), 1)
    flipped = packed.T
    work_ref[:, :width] = jnp.where(col <= row, packed, flipped)
    work_ref[:, width:] = jnp.where(col == row, 1.0, 0.0)
    size = 64
    for k in range(0, width, size):
        tile = k // 128 * 128
        block = inverse_of_block(work_ref[k : k + size, tile : tile + 128], k - tile, size)
        rows = matmul(block, work_ref[k : k + size, :], (1, 0))
        inverse_ref[k : k + size, :] = rows[:, width:]
        if k + size < width:
            below = matmul(rows[:, k + size : width], rows, (0, 0))
            work_ref[k + size :, :] = work_ref[k + size :, :] - below
    cross = jnp.where(col > row, packed, jnp.where(col == row, diagonal, flipped))
    inverse = inverse_ref[...]
    whole_inverse = matmul(inverse, inverse, (0, 0))
    product = jnp.concatenate([gathered_ref[2 * (j % 8) + j // 8, :BLOCK] for j in range(16)], 0)
    basis_ref[...] = matmul(panel, inverse, (0, 1))
    left = matmul(panel, whole_inverse, (0, 0))
    left_ref[:, :width] = left
    left_ref[:, width:] = matmul(product - matmul(left, cross, (1, 0)), whole_inverse, (1, 0))


def finish(gathered, panel):
    width, rows = panel.shape
    return pl.pallas_call(
        finish_kernel,
        out_shape=(
            jax.ShapeDtypeStruct((rows, width), jnp.float32),
            jax.ShapeDtypeStruct((rows, 2 * width), jnp.float32),
        ),
        scratch_shapes=[
            pltpu.VMEM((width, 2 * width), jnp.float32),
            pltpu.VMEM((width, width), jnp.float32),
        ],
        compiler_params=pltpu.CompilerParams(vmem_limit_bytes=32 * 2**20),
        cost_estimate=pl.CostEstimate(flops=2 * 10**9, bytes_accessed=4 * 10**6, transcendentals=0),
        name="finish",
    )(gathered, panel)


def exchange(value, axis):
    return lax.all_to_all(value, axis, 0, 0, tiled=True)


def repeat(value, count):
    return jnp.broadcast_to(value[None], (count, *value.shape))


def blocks_of_columns():
    pairs = []
    for z in range(8):
        for x in range(4):
            for col in range(16):
                row = 2 * col + x // 2
                source = 2 * z + x % 2
                pairs.append((row * 16 + source, (z * 4 + x) * 16 + col))
    return pairs


def shards(trailing, panel):
    width = panel.shape[1] * lax.axis_size(COLS)
    place = 8 * lax.axis_index("c") + lax.axis_index("y")
    pairs = blocks_of_columns()
    high = lax.Precision.HIGH

    panel_rows = lax.all_gather(panel, COLS, axis=1, tiled=True)
    block = lax.dynamic_slice(panel_rows, (place * BLOCK, 0), (BLOCK, width))
    panel_block = lax.ppermute(block, ALL, pairs)

    partial = matmul(trailing, panel_rows, (0, 0), high)
    partial = exchange(partial.reshape(4, 256, width), "x")
    partial, panel_block = lax.optimization_barrier((partial, panel_block))
    partial = partial.sum(0)
    product_block = exchange(partial.reshape(8, BLOCK, width), "z").sum(0)

    both = jnp.concatenate([product_block, panel_block], 1)
    both = exchange(repeat(both, 8), "z").reshape(256, 2 * width)
    both_cols = exchange(repeat(both, 4), "x").reshape(1024, 2 * width)

    back = lax.ppermute(product_block, ALL, [(b, a) for a, b in pairs])

    small = matmul(both_cols[:, width:], both_cols, (0, 0))
    cross, gram = small[:, :width], small[:, width:]
    row, col = iota((width, width), 0), iota((width, width), 1)
    packed = jnp.where(col <= row, gram, cross).reshape(16, 16, width)
    diagonal = jnp.sum(jnp.where(col == row, cross, 0.0), 0)
    own = iota((16, 1, width), 0) == iota((16, 1, width), 2) // 16
    packed = jnp.concatenate([packed, jnp.where(own, diagonal, 0.0)], 1)
    packed = packed.reshape(8, 2, 17, width).transpose(1, 0, 2, 3)
    packed, back = lax.optimization_barrier((packed, back))
    packed = exchange(packed, "c").sum(0)
    packed = exchange(packed, "y").sum(0)

    gathered = lax.all_gather(jnp.concatenate([back, packed], 0), COLS, axis=0)
    basis_rows, left = finish(gathered, panel_rows.T)
    updated = trailing - matmul(left, both_cols, (1, 1), high)
    return (updated, basis_rows)


def solution(mesh):
    fine = Mesh(mesh.devices.reshape(8, 4, 8, 2), ALL)
    return jax.shard_map(
        shards, mesh=fine, in_specs=(P(ROWS, COLS), P(ROWS, COLS)),
        out_specs=(P(ROWS, COLS), P(ROWS, None)), check_vma=False,
    )
```

```python
import jax
import jax.numpy as jnp
from jax import lax
from jax.experimental import pallas as pl
from jax.experimental.pallas import tpu as pltpu
from jax.sharding import Mesh, PartitionSpec as P

ROWS = ("z", "x")
COLS = ("y", "c")
ALL = ("z", "x", "y", "c")
BLOCK = 32


def matmul(left, right, contract, precision=lax.Precision.HIGHEST):
    return lax.dot_general(
        left, right, ((contract[:1], contract[1:]), ((), ())),
        precision=precision, preferred_element_type=jnp.float32,
    )


def split(value):
    top = value.astype(jnp.bfloat16)
    return top, (value - top.astype(jnp.float32)).astype(jnp.bfloat16)


def matmul3(left, right, contract):
    (a, b), (c, d) = split(left), split(right)
    low = matmul(a, d, contract, None) + matmul(b, c, contract, None)
    return matmul(a, c, contract, None) + low


def partial_kernel(panel_ref, trailing_ref, out_ref):
    out_ref[...] = matmul3(panel_ref[...], trailing_ref[...], (1, 0)).T


def partial_product(panel, trailing):
    (width, rows), columns = panel.shape, trailing.shape[1]
    return pl.pallas_call(
        partial_kernel,
        grid=(columns // 256,),
        in_specs=[
            pl.BlockSpec((width, rows), lambda i: (0, 0)),
            pl.BlockSpec((rows, 256), lambda i: (0, i)),
        ],
        out_specs=pl.BlockSpec((256, width), lambda i: (i, 0)),
        out_shape=jax.ShapeDtypeStruct((columns, width), jnp.float32),
        compiler_params=pltpu.CompilerParams(vmem_limit_bytes=60 * 2**20),
        cost_estimate=pl.CostEstimate(flops=8 * 10**8, bytes_accessed=4 * 10**6, transcendentals=0),
        name="partial_product",
    )(panel, trailing)


def iota(shape, dimension):
    return lax.broadcasted_iota(jnp.int32, shape, dimension)


def whole(value):
    return jnp.broadcast_to(value, (8, 128))


def inverse_of_block(tile, offset, size):
    start = 0 if offset else size
    lane, row = iota((size, 128), 1), iota((size, 128), 0)
    inside = (lane >= offset) & (lane < offset + size)
    work = jnp.where(inside, tile, jnp.where(lane == row + start, 1.0, 0.0))
    count = size // 8
    parts = [work[8 * i : 8 * i + 8] for i in range(count)]
    sub = iota((8, 128), 0)
    done = []
    for q in range(count):
        first = offset + 8 * q
        cols = [
            [whole(part[:, first + j : first + j + 1]) for j in range(8)]
            for part in parts[q:]
        ]
        pivots = {(i, j): whole(cols[0][j][i : i + 1]) for j in range(8) for i in range(j, 8)}
        rows = [whole(parts[q][i : i + 1]) for i in range(8)]
        inverses = []
        for j in range(8):
            inverses.append(1.0 / pivots[j, j])
            factors = {i: pivots[i, j] * inverses[j] for i in range(j + 1, 8)}
            for m in range(j + 1, 8):
                for i in range(m, 8):
                    pivots[i, m] = pivots[i, m] - pivots[i, j] * pivots[m, j] * inverses[j]
            for i in range(j + 1, 8):
                rows[i] = rows[i] - factors[i] * rows[j]
                for part in cols[1:]:
                    part[i] = part[i] - factors[i] * part[j]
        scaled = [row_j * inverse for row_j, inverse in zip(rows, inverses)]
        for i in range(q + 1, count):
            total = cols[i - q][0] * scaled[0]
            for j in range(1, 8):
                total = total + cols[i - q][j] * scaled[j]
            parts[i] = parts[i] - total
        final = rows[0] / jnp.sqrt(pivots[0, 0])
        for j in range(1, 8):
            final = jnp.where(sub == j, rows[j] / jnp.sqrt(pivots[j, j]), final)
        done.append(final)
    return jnp.concatenate(done, 0)[:, start : start + size]


def finish_kernel(gathered_ref, panel_ref, basis_ref, left_ref, work_ref, inverse_ref):
    width = panel_ref.shape[0]
    panel = panel_ref[...]
    packed = jnp.concatenate([gathered_ref[j, BLOCK : BLOCK + 16] for j in range(16)], 0)
    diagonal = gathered_ref[0, BLOCK + 16 : BLOCK + 17]
    for j in range(1, 16):
        diagonal = diagonal + gathered_ref[j, BLOCK + 16 : BLOCK + 17]
    row, col = iota((width, width), 0), iota((width, width), 1)
    flipped = packed.T
    work_ref[:, :width] = jnp.where(col <= row, packed, flipped)
    work_ref[:, width:] = jnp.where(col == row, 1.0, 0.0)
    size = 64
    for k in range(0, width, size):
        tile = k // 128 * 128
        block = inverse_of_block(work_ref[k : k + size, tile : tile + 128], k - tile, size)
        rows = matmul(block, work_ref[k : k + size, :], (1, 0))
        inverse_ref[k : k + size, :] = rows[:, width:]
        if k + size < width:
            below = matmul(rows[:, k + size : width], rows, (0, 0))
            work_ref[k + size :, :] = work_ref[k + size :, :] - below
    cross = jnp.where(col > row, packed, jnp.where(col == row, diagonal, flipped))
    inverse = inverse_ref[...]
    whole_inverse = matmul(inverse, inverse, (0, 0))
    product = jnp.concatenate([gathered_ref[2 * (j % 8) + j // 8, :BLOCK] for j in range(16)], 0)
    basis_ref[...] = matmul(panel, inverse, (0, 1))
    left = matmul(panel, whole_inverse, (0, 0))
    left_ref[:, :width] = left
    left_ref[:, width:] = matmul(product - matmul(left, cross, (1, 0)), whole_inverse, (1, 0))


def finish(gathered, panel):
    width, rows = panel.shape
    return pl.pallas_call(
        finish_kernel,
        out_shape=(
            jax.ShapeDtypeStruct((rows, width), jnp.float32),
            jax.ShapeDtypeStruct((rows, 2 * width), jnp.float32),
        ),
        scratch_shapes=[
            pltpu.VMEM((width, 2 * width), jnp.float32),
            pltpu.VMEM((width, width), jnp.float32),
        ],
        compiler_params=pltpu.CompilerParams(vmem_limit_bytes=32 * 2**20),
        cost_estimate=pl.CostEstimate(flops=2 * 10**9, bytes_accessed=4 * 10**6, transcendentals=0),
        name="finish",
    )(gathered, panel)


def exchange(value, axis):
    return lax.all_to_all(value, axis, 0, 0, tiled=True)


def repeat(value, count):
    return jnp.broadcast_to(value[None], (count, *value.shape))


def blocks_of_columns():
    pairs = []
    for z in range(8):
        for x in range(4):
            for col in range(16):
                row = 2 * col + x // 2
                source = 2 * z + x % 2
                pairs.append((row * 16 + source, (z * 4 + x) * 16 + col))
    return pairs


def shards(trailing, panel):
    width = panel.shape[1] * lax.axis_size(COLS)
    place = 8 * lax.axis_index("c") + lax.axis_index("y")
    pairs = blocks_of_columns()
    high = lax.Precision.HIGH

    panel_rows = lax.all_gather(panel, COLS, axis=1, tiled=True)
    block = lax.dynamic_slice(panel_rows, (place * BLOCK, 0), (BLOCK, width))
    panel_block = lax.ppermute(block, ALL, pairs)

    partial = partial_product(panel_rows.T, trailing)
    partial = exchange(partial.reshape(4, 256, width), "x")
    partial, panel_block = lax.optimization_barrier((partial, panel_block))
    partial = partial.sum(0)
    product_block = exchange(partial.reshape(8, BLOCK, width), "z").sum(0)

    both = jnp.concatenate([product_block, panel_block], 1)
    both = exchange(repeat(both, 8), "z").reshape(256, 2 * width)
    both_cols = exchange(repeat(both, 4), "x").reshape(1024, 2 * width)

    back = lax.ppermute(product_block, ALL, [(b, a) for a, b in pairs])

    small = matmul(both_cols[:, width:], both_cols, (0, 0))
    cross, gram = small[:, :width], small[:, width:]
    row, col = iota((width, width), 0), iota((width, width), 1)
    packed = jnp.where(col <= row, gram, cross).reshape(16, 16, width)
    diagonal = jnp.sum(jnp.where(col == row, cross, 0.0), 0)
    own = iota((16, 1, width), 0) == iota((16, 1, width), 2) // 16
    packed = jnp.concatenate([packed, jnp.where(own, diagonal, 0.0)], 1)
    packed = packed.reshape(8, 2, 17, width).transpose(1, 0, 2, 3)
    packed, back = lax.optimization_barrier((packed, back))
    packed = exchange(packed, "c").sum(0)
    packed = exchange(packed, "y").sum(0)

    gathered = lax.all_gather(jnp.concatenate([back, packed], 0), COLS, axis=0)
    basis_rows, left = finish(gathered, panel_rows.T)
    updated = trailing - matmul(left, both_cols, (1, 1), high)
    return (updated, basis_rows)


def solution(mesh):
    fine = Mesh(mesh.devices.reshape(8, 4, 8, 2), ALL)
    return jax.shard_map(
        shards, mesh=fine, in_specs=(P(ROWS, COLS), P(ROWS, COLS)),
        out_specs=(P(ROWS, COLS), P(ROWS, None)), check_vma=False,
    )
```
